32 devices in a mesh: shot: 8 (over y, x, core), space: 4 (over z).
Axes of the slice: x: 2, y: 2, z: 4, core: 2. Of those that a mesh axis runs over, the one named last changes fastest.
Arguments:
- courant: float32 [32, 128, 128], P('space'), may hold values from 0.03 to 0.18
- checkpoint: float32 [8, 2, 512, 8, 128], P('shot', None, 'space'), may hold values from -6 to 6
- block_target: int32 [8, 512], P('shot'), may hold values from 0 to 511, as said below
- adjoint_state: float32 [8, 2, 32, 128, 128], P('shot', None, 'space'), may hold values from -6 to 6
- wavelet: float32 [8, 4], P('shot'), may hold values from -8 to 8
- source_cell: int32 [8], P('shot'), may hold values from 0 to 524287
- receiver_cell: int32 [8, 512], P('shot'), may hold values from 0 to 524287
- residual: float32 [8, 4, 512], P('shot'), may hold values from -6 to 6
- check_rows: int32 [4, 64, 16], P('space'), may hold values from 0 to 1023
Outputs:
- gradient: float32 [32, 128, 128], P('space', 'shot')
- adjoint_carry: float32 [8, 2, 32, 128, 128], P('shot', None, 'space')
- checksums: float32 [4, 64, 128], P('space', 'shot')
The draws below stay inside these ranges and needn't reach their ends.
Inputs may be any that keep to these rules, and one draw needn't show every extreme that they name: `block_target`: each shot's row is a permutation of the block positions. The stored blocks of one device (aligned blocks of 128 entries) name at most 32 positions of any one slab (128 consecutive positions); each device names exactly 32 of one slab, and each slab is named exactly 32 times by one device.
All inputs are finite; a program needn't handle non-finite values.
Results may differ from the reference program's by a relative error of at most 0.0003.
Values sent between devices are 32-bit elements; how exact they have to be, the bound alone decides.
A program may use at most 128 MiB of HBM per device.

```python
import math
import jax
import jax.numpy as jnp
from jax import lax

CX = 8
NY = 128
NZ = 128
NREC = 512
BY = 8
NT = 4
KSEL = 16
NX = 32
SHOTS = 8
BLK_DEV = 128
NBLK = 512
CAP = 32
CHK_SLAB = 64
N_SPACE = 4


def one_target(subkey):
    readers = NBLK // BLK_DEV
    key_shift, key_read, key_send = jax.random.split(subkey, 3)
    shifts = jax.random.permutation(key_shift, readers)
    remainder = BLK_DEV - CAP
    ranking = jnp.arange(readers, dtype=jnp.int32)
    weights = jnp.where(ranking == 0, CAP, remainder // (readers - 1) + (ranking - 1 < remainder % (readers - 1)).astype(jnp.int32)).astype(jnp.int32)
    by_shift = jnp.zeros((readers,), jnp.int32).at[shifts].set(weights)
    senders = jnp.arange(readers, dtype=jnp.int32)
    counts = by_shift[(senders[None, :] - senders[:, None]) % readers]
    send_end = jnp.cumsum(counts, axis=1)
    send_start = send_end - counts
    take_end = jnp.cumsum(counts, axis=0)
    take_start = take_end - counts
    slot_ids = jnp.arange(BLK_DEV, dtype=jnp.int32)
    peer_of = jnp.sum((send_end[:, None, :] <= slot_ids[None, :, None]).astype(jnp.int32), axis=2)
    within = slot_ids[None, :] - jnp.take_along_axis(send_start, peer_of, axis=1)
    arrival = jnp.take_along_axis(take_start, peer_of, axis=1) + within
    read_perm = jax.vmap(lambda subject: jax.random.permutation(subject, BLK_DEV))(jax.random.split(key_read, readers))
    send_perm = jax.vmap(lambda subject: jax.random.permutation(subject, BLK_DEV))(jax.random.split(key_send, readers))
    local_block = read_perm[peer_of, arrival]
    global_block = peer_of * BLK_DEV + local_block
    placed = jnp.zeros((readers, BLK_DEV), jnp.int32).at[senders[:, None], send_perm].set(global_block.astype(jnp.int32))
    return placed.reshape(-1)


def draw_block_target(key, part):
    return jax.vmap(one_target)(jax.random.split(key, SHOTS))


def plant(values, own_key, low, top_value):
    dims = values.shape
    place = [jax.random.randint(jax.random.fold_in(own_key, axis), (), 0, dims[axis]) for axis in range(len(dims))]
    values = values.at[tuple(place)].set(low)
    longest = dims.index(max(dims))
    place[longest] = (place[longest] + 1) % dims[longest]
    return values.at[tuple(place)].set(top_value)


def shard_levels(own_key, shape, cuts, least, top_value):
    def one(axis_at, parts):
        heights = jax.random.uniform(jax.random.fold_in(jax.random.fold_in(own_key, 6), axis_at), (parts,), jnp.float32, least / len(cuts), top_value / len(cuts))
        return jnp.repeat(jnp.exp(heights), shape[axis_at] // parts).reshape((-1,) + (1,) * (len(shape) - axis_at - 1))

    factor_of = one(*cuts[0])
    for cut in cuts[1:]:
        factor_of = factor_of * one(*cut)
    return factor_of


def noise(own_key, extent, width, limit, shards=(), kind=jnp.bfloat16):
    loudness = shard_levels(own_key, extent, shards, -0.22, 0.18) if shards else 1.0
    values = jax.random.normal(own_key, extent, jnp.float32) * width * loudness
    return jnp.minimum(jnp.maximum(values, -limit), limit).astype(kind)


def setup_inputs(seed: int = 0) -> dict:
    streams_of = jax.random.split(jax.random.key(seed), 10)
    return {
        "courant": jnp.clip(jnp.exp(math.log(0.18) - 1.7917595 * jax.random.uniform(streams_of[0], (NX, NY, NZ), jnp.float32) ** shard_levels(streams_of[0], (NX, NY, NZ), ((0, 4),), -0.2, 0.2)), 0.03, 0.18),
        "checkpoint": noise(streams_of[1], (SHOTS, 2, NBLK, BY, NZ), 1.0, 6.0, ((0, 8), (2, 4)), jnp.float32),
        "block_target": draw_block_target(jax.random.fold_in(streams_of[9], 71), 0),
        "adjoint_state": noise(streams_of[3], (SHOTS, 2, NX, NY, NZ), 1.0, 6.0, ((0, 8), (2, 4)), jnp.float32),
        "wavelet": noise(streams_of[4], (SHOTS, NT), 2.0, 8.0, ((0, 8),), jnp.float32),
        "source_cell": plant(jax.random.randint(streams_of[5], (SHOTS,), 0, NX * NY * NZ), jax.random.fold_in(streams_of[5], 1), 0, (NX * NY * NZ) - 1).astype(jnp.int32),
        "receiver_cell": plant(jax.random.randint(streams_of[6], (SHOTS, NREC), 0, NX * NY * NZ), jax.random.fold_in(streams_of[6], 1), 0, (NX * NY * NZ) - 1).astype(jnp.int32),
        "residual": noise(streams_of[7], (SHOTS, NT, NREC), 1.0, 6.0, ((0, 8),), jnp.float32),
        "check_rows": plant(jax.random.randint(streams_of[8], (N_SPACE, CHK_SLAB, KSEL), 0, CX * NY), jax.random.fold_in(streams_of[8], 1), 0, (CX * NY) - 1).astype(jnp.int32),
    }


STENCIL = (-205.0 / 72.0, 8.0 / 5.0, -1.0 / 5.0, 8.0 / 315.0, -1.0 / 560.0)


def laplace(field):
    length = field.shape[0] - 8
    height = field.shape[1]
    breadth = field.shape[2]
    padded = jnp.pad(field, ((0, 0), (4, 4), (4, 4)))
    summed = (3.0 * STENCIL[0]) * padded[4:4 + length, 4:4 + height, 4:4 + breadth]
    for offset in range(1, 5):
        summed = summed + STENCIL[offset] * (padded[4 + offset:4 + offset + length, 4:4 + height, 4:4 + breadth] + padded[4 - offset:4 - offset + length, 4:4 + height, 4:4 + breadth])
    for offset in range(1, 5):
        summed = summed + STENCIL[offset] * (padded[4:4 + length, 4 + offset:4 + offset + height, 4:4 + breadth] + padded[4:4 + length, 4 - offset:4 - offset + height, 4:4 + breadth])
    for offset in range(1, 5):
        summed = summed + STENCIL[offset] * (padded[4:4 + length, 4:4 + height, 4 + offset:4 + offset + breadth] + padded[4:4 + length, 4:4 + height, 4 - offset:4 - offset + breadth])
    return summed


def inject(field, cell_index, values, first_row):
    plane_cells = field.shape[1] * field.shape[2]
    local_cell = cell_index - first_row * plane_cells
    inside = (local_cell >= 0) & (local_cell < field.shape[0] * plane_cells)
    target = jnp.where(inside, local_cell, field.shape[0] * plane_cells)
    flattened = field.reshape(-1).at[target].add(values, mode="drop")
    return flattened.reshape(field.shape)


def advance(before, current_ext, courant, wave_value, source, first_row):
    following = 2.0 * current_ext[4:-4] - before + courant * laplace(current_ext)
    return inject(following, source, wave_value, first_row)


def retreat(following, current, weighted_ext, values, cell_index, first_row):
    earlier = 2.0 * current - following + laplace(weighted_ext)
    return inject(earlier, cell_index, values, first_row)


def pad_planes(field):
    return jnp.pad(field, ((4, 4), (0, 0), (0, 0)))


def pick_sum(slab_rows, chosen):
    return jnp.sum(slab_rows[chosen], axis=1)


def reference(courant, checkpoint, block_target, adjoint_state, wavelet, source_cell, receiver_cell, residual, check_rows):
    def one_shot(running, inputs):
        blocks, target, carried, wavelet_row, source, receivers, traces = inputs
        placed = jnp.zeros_like(blocks).at[:, target].set(blocks)
        levels = placed.reshape(2, NX, NY, NZ)
        fields = [levels[0], levels[1]]
        for moment in range(1, NT + 1):
            fields.append(advance(fields[-2], pad_planes(fields[-1]), courant, wavelet_row[moment - 1:moment], source.reshape(1), 0))
        adjoints = [None] * (NT + 2)
        adjoints[NT + 1] = carried[0]
        adjoints[NT] = carried[1]
        for moment in range(NT, 0, -1):
            weighted = pad_planes(courant * adjoints[moment])
            adjoints[moment - 1] = retreat(adjoints[moment + 1], adjoints[moment], weighted, traces[moment - 1], receivers, 0)
        partial_value = jnp.zeros((NX, NY, NZ), jnp.float32)
        for moment in range(1, NT + 1):
            partial_value = partial_value + adjoints[moment] * ((fields[moment + 1] - 2.0 * fields[moment]) + fields[moment - 1])
        return running + partial_value, jnp.stack([adjoints[1], adjoints[0]])

    gradient, adjoint_carry = lax.scan(one_shot, jnp.zeros((NX, NY, NZ), jnp.float32), (checkpoint, block_target, adjoint_state, wavelet, source_cell, receiver_cell, residual))
    slab_view = gradient.reshape(N_SPACE, CX * NY, NZ)
    checksums = jax.vmap(pick_sum)(slab_view, check_rows)
    return gradient, adjoint_carry, checksums
```

```python
import functools

import jax
import jax.numpy as jnp
import ml_dtypes
import numpy as np
from jax import lax
from jax.experimental import pallas as pl
from jax.experimental.pallas import tpu as pltpu
from jax.sharding import PartitionSpec as P

STENCIL = (-205.0 / 72.0, 8.0 / 5.0, -1.0 / 5.0, 8.0 / 315.0, -1.0 / 560.0)
BF = jnp.bfloat16
F32 = jnp.float32
MESH = pl.DeviceIdType.MESH


def halves(value):
    high = float(np.asarray(value, ml_dtypes.bfloat16))
    low = float(np.asarray(value - high, ml_dtypes.bfloat16))
    return high, low


def split(value):
    high = value.astype(BF)
    return high, (value - high.astype(F32)).astype(BF)


def band(size, part, centre):
    gap = jnp.abs(
        lax.broadcasted_iota(jnp.int32, (size, size), 0)
        - lax.broadcasted_iota(jnp.int32, (size, size), 1)
    )
    out = jnp.zeros((size, size), F32)
    if centre:
        out = jnp.where(gap == 0, halves(3.0 * STENCIL[0])[part], out)
    for k in range(1, 5):
        out = jnp.where(gap == k, halves(STENCIL[k])[part], out)
    return out.astype(BF)


def dot(a, b):
    return jnp.dot(a, b, preferred_element_type=F32)


def kernel(
    n, shots, cap,
    pack, where, source, wave,
    courant, blocks, adj, receivers, residual, check_rows,
    grad_out, carry, check_out,
    fp, fw, halo, p0, q3, q2, aq, dp, inj, grad, check, rs, rs_check,
    out1, out0, in1, in0, wz, wy, bt,
    halo_send, halo_recv, a2a_send, a2a_recv, rs_send, rs_recv,
):
    steps = residual.shape[0]
    length, height, breadth = courant.shape
    nrec = residual.shape[1]
    pos = lax.axis_index("space")
    shot = lax.axis_index("shot")
    rows = height // shots
    check_each = check_rows.shape[0] // shots

    barrier = pltpu.get_barrier_semaphore()
    for off in range(1, n):
        pl.semaphore_signal(
            barrier, inc=1, device_id={"space": lax.rem(pos + off, n)}, device_id_type=MESH
        )
    for off in range(1, shots):
        pl.semaphore_signal(
            barrier, inc=1, device_id={"shot": lax.rem(shot + off, shots)}, device_id_type=MESH
        )

    def halo_copy(chain, level, side):
        src = (fp, fw)[chain]
        first = 4 if side == 0 else 8
        peer = lax.rem(pos + (n - 1 if side == 0 else 1), n)
        return pltpu.make_async_remote_copy(
            src_ref=src.at[level, pl.ds(first, 4)],
            dst_ref=halo.at[chain, level, 1 - side],
            send_sem=halo_send.at[chain, level, side],
            recv_sem=halo_recv.at[chain, level, 1 - side],
            device_id={"space": peer},
            device_id_type=MESH,
        )

    def has(side):
        return pos > 0 if side == 0 else pos < n - 1

    def send_halo(chain, level, side):
        @pl.when(has(side))
        def _():
            halo_copy(chain, level, side).start()

    def wait_halo(chain, level, side):
        @pl.when(has(side))
        def _():
            halo_copy(chain, level, 1 - side).wait_recv()

    def wait_sent(chain, level, side):
        @pl.when(has(side))
        def _():
            halo_copy(chain, level, side).wait_send()

    def a2a_copy(level, off):
        src, dst = ((out0, in0), (out1, in1))[level]
        return pltpu.make_async_remote_copy(
            src_ref=src.at[pl.ds(off * cap, cap)],
            dst_ref=dst.at[pl.ds(off * cap, cap)],
            send_sem=a2a_send.at[level, off],
            recv_sem=a2a_recv.at[level, off],
            device_id={"space": lax.rem(pos + off, n)},
            device_id_type=MESH,
        )

    def first_weight(x, c):
        fw[0, x + 4] = courant[x] * adj[1, x]
        return c

    lax.fori_loop(0, length, first_weight, 0)

    def do_pack(level):
        src, dst = ((out0, in0), (out1, in1))[level]

        def own(i, c):
            for u in range(8):
                dst[i * 8 + u] = blocks[level, pack[i * 8 + u]]
            return c

        def other(i, c):
            for u in range(8):
                src[i * 8 + u] = blocks[level, pack[i * 8 + u]]
            return c

        lax.fori_loop(0, cap // 8, own, 0)
        lax.fori_loop(cap // 8, n * cap // 8, other, 0)

    do_pack(1)
    pl.semaphore_wait(barrier, n - 1 + shots - 1)
    for side in range(2):
        send_halo(1, 0, side)
    for off in range(1, n):
        a2a_copy(1, off).start()
    do_pack(0)
    for off in range(1, n):
        a2a_copy(0, off).start()

    def zero(i, c):
        blank = jnp.zeros((height, breadth), F32)
        for level in range(steps):
            for f in (fp, fw):
                f[level, i] = blank
                f[level, i + 4 + length] = blank
        return c

    lax.fori_loop(0, 4, zero, 0)
    for side in range(2):
        @pl.when(jnp.logical_not(has(side)))
        def _():
            def blank(i, c):
                for level in range(steps):
                    for chain in range(2):
                        halo[chain, level, side, i] = jnp.zeros((height, breadth), F32)
                return c

            lax.fori_loop(0, 4, blank, 0)

    for part in range(2):
        z = band(breadth, part, True)
        y = band(height, part, False)
        for k in range(2):
            wz[k * breadth:(k + 1) * breadth, part * breadth:(part + 1) * breadth] = z
            wy[part * height:(part + 1) * height, k * height:(k + 1) * height] = y

    local = receivers[...] - pos * (length * height * breadth)
    rec_row = local // breadth
    rec_col = local - rec_row * breadth
    column = lax.broadcasted_iota(jnp.int32, (breadth, nrec), 0) == rec_col
    for s in range(steps):
        value = residual[s:s + 1, :]
        high = value.astype(BF).astype(F32)
        for k, v in enumerate((high, value - high)):
            bt[s * breadth:(s + 1) * breadth, k * nrec:(k + 1) * nrec] = jnp.where(
                column, v, 0.0
            ).astype(BF)

    def fill_inj(x, c):
        line = lax.broadcasted_iota(jnp.int32, (height, nrec), 0) + x * height
        hot = jnp.where(line == rec_row, 1.0, 0.0).astype(BF)
        got = lax.dot_general(
            jnp.concatenate([hot, hot], axis=1), bt[...], (((1,), (1,)), ((), ())),
            preferred_element_type=F32,
        )
        for s in range(steps):
            inj[s, x] = got[:, s * breadth:(s + 1) * breadth]
        return c

    lax.fori_loop(0, length, fill_inj, 0)

    def spatial(f, level, x):
        plane = f[level, x + 4]
        high, low = split(plane)
        oz = dot(jnp.concatenate([high, low], axis=1), wz[...])
        oy = dot(wy[...], jnp.concatenate([high, low], axis=0))
        acc = (oz[:, :breadth] + oz[:, breadth:]) + (oy[:height] + oy[height:])
        for k in range(1, 5):
            acc = acc + STENCIL[k] * (f[level, x + 4 + k] + f[level, x + 4 - k])
        return acc

    qs = [adj.at[0], adj.at[1]]
    for m in range(steps - 2):
        qs.append((q3, q2)[m] if m < 2 else None)
    qs += [carry.at[0], carry.at[1]]

    def prep_q(level):
        def one(x, c):
            aq[x] = (
                (2.0 * qs[level + 1][x] - qs[level][x])
                + inj[steps - 1 - level, x]
                + spatial(fw, level, x)
            )
            return c

        lax.fori_loop(0, length, one, 0, unroll=2)

    src_local = source[0] - pos * (length * height * breadth)

    def prep_p(level):
        flat = (
            lax.broadcasted_iota(jnp.int32, (height, breadth), 0) * breadth
            + lax.broadcasted_iota(jnp.int32, (height, breadth), 1)
        )
        amount = wave[level]

        def one(x, c):
            hit = flat == src_local - x * (height * breadth)
            dp[level, x] = courant[x] * spatial(fp, level, x) + jnp.where(hit, amount, 0.0)
            return c

        lax.fori_loop(0, length, one, 0, unroll=2)

    def beyond(chain, level, side, i):
        total = None
        for k in range(i + 1, 5):
            at = 4 + i - k if side == 0 else k - i - 1
            term = STENCIL[k] * halo[chain, level, side, at]
            total = term if total is None else total + term
        return total

    def finish_q(level):
        for side in range(2):
            wait_halo(1, level, side)
            for i in range(4):
                x = i if side == 0 else length - 1 - i
                value = aq[x] + beyond(1, level, side, i)
                qs[level + 2][x] = value
                if level + 1 < steps:
                    fw[level + 1, x + 4] = courant[x] * value
            if level + 1 < steps:
                send_halo(1, level + 1, side)

    def finish_p(level):
        for side in range(2):
            wait_halo(0, level, side)
            for i in range(4):
                x = i if side == 0 else length - 1 - i
                change = dp[level, x] + courant[x] * beyond(0, level, side, i)
                if level + 1 < steps:
                    dp[level, x] = change
                    older = p0[x] if level == 0 else fp[level - 1, x + 4]
                    fp[level + 1, x + 4] = (2.0 * fp[level, x + 4] - older) + change
                else:
                    grad[x] = grad[x] + qs[1][x] * change
            if level + 1 < steps:
                send_halo(0, level + 1, side)

    def unpack(level, store):
        got = (in0, in1)[level]
        for off in range(1, n):
            a2a_copy(level, off).wait_recv()
        per_plane = height // 8

        def one(x, c):
            for r in range(per_plane):
                store(x, r, got[where[x * per_plane + r]])
            return c

        lax.fori_loop(0, length, one, 0)

    def store1(x, r, value):
        fp[0, x + 4, r * 8:(r + 1) * 8, :] = value

    def store0(x, r, value):
        p0[x, r * 8:(r + 1) * 8, :] = value

    prep_q(0)
    finish_q(0)
    unpack(1, store1)
    for side in range(2):
        send_halo(0, 0, side)
    prep_q(1)
    prep_p(0)
    finish_q(1)
    prep_q(2)
    unpack(0, store0)
    for level in range(steps - 1):
        finish_p(level)
        prep_p(level + 1)
        if level + 2 < steps - 1:
            finish_q(level + 2)
            prep_q(level + 3)

    def early(x, c):
        total = qs[steps][x] * dp[0, x]
        for m in range(1, steps - 1):
            total = total + qs[steps - m][x] * dp[m, x]
        grad[x] = total
        return c

    lax.fori_loop(0, length, early, 0)

    line = lax.broadcasted_iota(jnp.int32, (check_rows.shape[0], length * height), 1)
    chosen = check_rows[...]
    counts = jnp.zeros(line.shape, F32)
    for k in range(chosen.shape[1]):
        counts = counts + jnp.where(line == chosen[:, k:k + 1], 1.0, 0.0)
    counts = counts.astype(BF)

    finish_p(steps - 1)

    def rs_copy(off):
        peer = lax.rem(shot + off, shots)
        return pltpu.make_async_remote_copy(
            src_ref=grad.at[:, pl.ds(pl.multiple_of(peer * rows, rows), rows), :],
            dst_ref=rs.at[off],
            send_sem=rs_send.at[0, off],
            recv_sem=rs_recv.at[0, off],
            device_id={"shot": peer},
            device_id_type=MESH,
        )

    def rs_check_copy(off):
        peer = lax.rem(shot + off, shots)
        return pltpu.make_async_remote_copy(
            src_ref=check.at[pl.ds(pl.multiple_of(peer * check_each, check_each), check_each), :],
            dst_ref=rs_check.at[off],
            send_sem=rs_send.at[1, off],
            recv_sem=rs_recv.at[1, off],
            device_id={"shot": peer},
            device_id_type=MESH,
        )

    for off in range(1, shots):
        rs_copy(off).start()
    high, low = split(grad[...].reshape(length * height, breadth))
    both = dot(counts, jnp.concatenate([high, low], axis=1))
    check[...] = both[:, :breadth] + both[:, breadth:]
    for off in range(1, shots):
        rs_check_copy(off).start()

    finish_q(steps - 1)

    total = grad[:, pl.ds(pl.multiple_of(shot * rows, rows), rows), :]
    for off in range(1, shots):
        rs_copy(off).wait_recv()
        total = total + rs[off]
    grad_out[...] = total
    total = check[pl.ds(pl.multiple_of(shot * check_each, check_each), check_each), :]
    for off in range(1, shots):
        rs_check_copy(off).wait_recv()
        total = total + rs_check[off]
    check_out[...] = total

    for chain in range(2):
        for level in range(steps):
            for side in range(2):
                wait_sent(chain, level, side)
    for level in range(2):
        for off in range(1, n):
            a2a_copy(level, off).wait_send()
    for off in range(1, shots):
        rs_copy(off).wait_send()
        rs_check_copy(off).wait_send()


def tables(targets, n, cap, per_device, pos):
    grid = targets.reshape(n, per_device)
    peers = grid // per_device
    order = jnp.arange(per_device, dtype=jnp.int32)
    same = (peers[:, :, None] == peers[:, None, :]) & (order[None, None, :] < order[None, :, None])
    rank = jnp.sum(same.astype(jnp.int32), axis=2)
    sender = jnp.arange(n, dtype=jnp.int32)[:, None]
    slot = ((peers - sender + n) % n) * cap + rank
    own = lax.dynamic_index_in_dim(slot, pos, 0, keepdims=False)
    slots = jnp.arange(n * cap, dtype=jnp.int32)
    pack = jnp.sum(jnp.where(own[None, :] == slots[:, None], order[None, :], 0), axis=1)
    mine = pos * per_device + order
    where = jnp.sum(
        jnp.where(targets[None, :] == mine[:, None], slot.reshape(1, -1), 0), axis=1
    )
    return pack, where


def body(
    courant, checkpoint, block_target, adjoint_state, wavelet, source_cell,
    receiver_cell, residual, check_rows,
):
    n = lax.axis_size("space")
    shots = lax.axis_size("shot")
    length, height, breadth = courant.shape
    per_device = checkpoint.shape[2]
    cap = per_device // 4
    steps = wavelet.shape[1]
    chk = check_rows.shape[1]
    nrec = residual.shape[2]
    pack, where = tables(block_target[0], n, cap, per_device, lax.axis_index("space"))

    smem = pl.BlockSpec(memory_space=pltpu.SMEM)
    vmem = pl.BlockSpec(memory_space=pltpu.VMEM)
    slab = (length, height, breadth)
    buf = lambda *shape: pltpu.VMEM(shape, F32)
    blk = checkpoint.shape[3:]
    dma = pltpu.SemaphoreType.DMA
    grad, carry, check = pl.pallas_call(
        functools.partial(kernel, n, shots, cap),
        out_shape=(
            jax.ShapeDtypeStruct((length, height // shots, breadth), F32),
            jax.ShapeDtypeStruct((2,) + slab, F32),
            jax.ShapeDtypeStruct((chk // shots, breadth), F32),
        ),
        in_specs=[smem] * 4 + [vmem] * 6,
        out_specs=(vmem,) * 3,
        scratch_shapes=[
            buf(steps, length + 8, height, breadth),
            buf(steps, length + 8, height, breadth),
            buf(2, steps, 2, 4, height, breadth),
            buf(*slab), buf(*slab), buf(*slab), buf(*slab),
            buf(steps, *slab), buf(steps, *slab), buf(*slab),
            buf(chk, breadth),
            buf(shots, length, height // shots, breadth),
            buf(shots, chk // shots, breadth),
            buf(n * cap, *blk), buf(n * cap, *blk), buf(n * cap, *blk), buf(n * cap, *blk),
            pltpu.VMEM((2 * breadth, 2 * breadth), BF),
            pltpu.VMEM((2 * height, 2 * height), BF),
            pltpu.VMEM((steps * breadth, 2 * nrec), BF),
            dma((2, steps, 2)), dma((2, steps, 2)),
            dma((2, n)), dma((2, n)), dma((2, shots)), dma((2, shots)),
        ],
        compiler_params=pltpu.CompilerParams(
            collective_id=0, has_side_effects=True, vmem_limit_bytes=56 * 1024 * 1024
        ),
    )(
        pack, where, source_cell, wavelet[0],
        courant, checkpoint[0], adjoint_state[0], receiver_cell, residual[0], check_rows[0],
    )
    return grad, carry[None], check[None]


def solution(mesh):
    in_specs = (
        P("space", None, None),
        P("shot", None, "space", None, None),
        P("shot", None),
        P("shot", None, "space", None, None),
        P("shot", None),
        P("shot"),
        P("shot", None),
        P("shot", None, None),
        P("space", None, None),
    )
    out_specs = (
        P("space", "shot", None),
        P("shot", None, "space", None, None),
        P("space", "shot", None),
    )
    return jax.shard_map(body, mesh=mesh, in_specs=in_specs, out_specs=out_specs, check_vma=False)
```

```python
import functools

import jax
import jax.numpy as jnp
import ml_dtypes
import numpy as np
from jax import lax
from jax.experimental import pallas as pl
from jax.experimental.pallas import tpu as pltpu
from jax.sharding import PartitionSpec as P

STENCIL = (-205.0 / 72.0, 8.0 / 5.0, -1.0 / 5.0, 8.0 / 315.0, -1.0 / 560.0)
BF = jnp.bfloat16
F32 = jnp.float32
MESH = pl.DeviceIdType.MESH


def halves(value):
    high = float(np.asarray(value, ml_dtypes.bfloat16))
    low = float(np.asarray(value - high, ml_dtypes.bfloat16))
    return high, low


def split(value):
    high = value.astype(BF)
    return high, (value - high.astype(F32)).astype(BF)


def band(size, part, centre):
    gap = jnp.abs(
        lax.broadcasted_iota(jnp.int32, (size, size), 0)
        - lax.broadcasted_iota(jnp.int32, (size, size), 1)
    )
    out = jnp.zeros((size, size), F32)
    if centre:
        out = jnp.where(gap == 0, halves(3.0 * STENCIL[0])[part], out)
    for k in range(1, 5):
        out = jnp.where(gap == k, halves(STENCIL[k])[part], out)
    return out.astype(BF)


def dot(a, b):
    return jnp.dot(a, b, preferred_element_type=F32)


def kernel(
    n, shots, cap,
    pack, where, source, wave,
    courant, blocks, adj, receivers, residual, check_rows,
    grad_out, carry, check_out,
    fp, fw, halo, p0, q3, q2, aq, dp, inj, grad, check, rs, rs_check,
    out1, out0, in1, in0, wz, wy, bt,
    halo_send, halo_recv, a2a_send, a2a_recv, rs_send, rs_recv,
):
    steps = residual.shape[0]
    length, height, breadth = courant.shape
    nrec = residual.shape[1]
    pos = lax.axis_index("space")
    shot = lax.axis_index("shot")
    rows = height // shots
    check_each = check_rows.shape[0] // shots

    barrier = pltpu.get_barrier_semaphore()
    for off in range(1, n):
        pl.semaphore_signal(
            barrier, inc=1, device_id={"space": lax.rem(pos + off, n)}, device_id_type=MESH
        )
    for off in range(1, shots):
        pl.semaphore_signal(
            barrier, inc=1, device_id={"shot": lax.rem(shot + off, shots)}, device_id_type=MESH
        )

    def halo_copy(chain, level, side):
        src = (fp, fw)[chain]
        first = 4 if side == 0 else 8
        peer = lax.rem(pos + (n - 1 if side == 0 else 1), n)
        return pltpu.make_async_remote_copy(
            src_ref=src.at[level, pl.ds(first, 4)],
            dst_ref=halo.at[chain, level, 1 - side],
            send_sem=halo_send.at[chain, level, side],
            recv_sem=halo_recv.at[chain, level, 1 - side],
            device_id={"space": peer},
            device_id_type=MESH,
        )

    def has(side):
        return pos > 0 if side == 0 else pos < n - 1

    def send_halo(chain, level, side):
        @pl.when(has(side))
        def _():
            halo_copy(chain, level, side).start()

    def wait_halo(chain, level, side):
        @pl.when(has(side))
        def _():
            halo_copy(chain, level, 1 - side).wait_recv()

    def wait_sent(chain, level, side):
        @pl.when(has(side))
        def _():
            halo_copy(chain, level, side).wait_send()

    def a2a_copy(level, off):
        src, dst = ((out0, in0), (out1, in1))[level]
        return pltpu.make_async_remote_copy(
            src_ref=src.at[pl.ds(off * cap, cap)],
            dst_ref=dst.at[pl.ds(off * cap, cap)],
            send_sem=a2a_send.at[level, off],
            recv_sem=a2a_recv.at[level, off],
            device_id={"space": lax.rem(pos + off, n)},
            device_id_type=MESH,
        )

    def first_weight(x, c):
        fw[0, x + 4] = courant[x] * adj[1, x]
        return c

    lax.fori_loop(0, length, first_weight, 0)

    def do_pack(level):
        src, dst = ((out0, in0), (out1, in1))[level]

        def own(i, c):
            for u in range(8):
                dst[i * 8 + u] = blocks[level, pack[i * 8 + u]]
            return c

        def other(i, c):
            for u in range(8):
                src[i * 8 + u] = blocks[level, pack[i * 8 + u]]
            return c

        lax.fori_loop(0, cap // 8, own, 0)
        lax.fori_loop(cap // 8, n * cap // 8, other, 0)

    do_pack(1)
    pl.semaphore_wait(barrier, n - 1 + shots - 1)
    for off in range(1, n):
        a2a_copy(1, off).start()
    for side in range(2):
        send_halo(1, 0, side)
    do_pack(0)
    for off in range(1, n):
        a2a_copy(0, off).start()

    def zero(i, c):
        blank = jnp.zeros((height, breadth), F32)
        for level in range(steps):
            for f in (fp, fw):
                f[level, i] = blank
                f[level, i + 4 + length] = blank
        return c

    lax.fori_loop(0, 4, zero, 0)
    for side in range(2):
        @pl.when(jnp.logical_not(has(side)))
        def _():
            def blank(i, c):
                for level in range(steps):
                    for chain in range(2):
                        halo[chain, level, side, i] = jnp.zeros((height, breadth), F32)
                return c

            lax.fori_loop(0, 4, blank, 0)

    for part in range(2):
        z = band(breadth, part, True)
        y = band(height, part, False)
        for k in range(2):
            wz[k * breadth:(k + 1) * breadth, part * breadth:(part + 1) * breadth] = z
            wy[part * height:(part + 1) * height, k * height:(k + 1) * height] = y

    local = receivers[...] - pos * (length * height * breadth)
    rec_row = local // breadth
    rec_col = local - rec_row * breadth
    column = lax.broadcasted_iota(jnp.int32, (breadth, nrec), 0) == rec_col
    for s in range(steps):
        value = residual[s:s + 1, :]
        high = value.astype(BF).astype(F32)
        for k, v in enumerate((high, value - high)):
            bt[s * breadth:(s + 1) * breadth, k * nrec:(k + 1) * nrec] = jnp.where(
                column, v, 0.0
            ).astype(BF)

    def fill_inj(x, c):
        line = lax.broadcasted_iota(jnp.int32, (height, nrec), 0) + x * height
        hot = jnp.where(line == rec_row, 1.0, 0.0).astype(BF)
        got = lax.dot_general(
            jnp.concatenate([hot, hot], axis=1), bt[...], (((1,), (1,)), ((), ())),
            preferred_element_type=F32,
        )
        for s in range(steps):
            inj[s, x] = got[:, s * breadth:(s + 1) * breadth]
        return c

    lax.fori_loop(0, length, fill_inj, 0)

    def spatial(f, level, x):
        plane = f[level, x + 4]
        high, low = split(plane)
        oz = dot(jnp.concatenate([high, low], axis=1), wz[...])
        oy = dot(wy[...], jnp.concatenate([high, low], axis=0))
        acc = (oz[:, :breadth] + oz[:, breadth:]) + (oy[:height] + oy[height:])
        for k in range(1, 5):
            acc = acc + STENCIL[k] * (f[level, x + 4 + k] + f[level, x + 4 - k])
        return acc

    qs = [adj.at[0], adj.at[1]]
    for m in range(steps - 2):
        qs.append((q3, q2)[m] if m < 2 else None)
    qs += [carry.at[0], carry.at[1]]

    def prep_q(level):
        def one(x, c):
            aq[x] = (
                (2.0 * qs[level + 1][x] - qs[level][x])
                + inj[steps - 1 - level, x]
                + spatial(fw, level, x)
            )
            return c

        lax.fori_loop(0, length, one, 0, unroll=2)

    src_local = source[0] - pos * (length * height * breadth)

    def prep_p(level):
        flat = (
            lax.broadcasted_iota(jnp.int32, (height, breadth), 0) * breadth
            + lax.broadcasted_iota(jnp.int32, (height, breadth), 1)
        )
        amount = wave[level]

        def one(x, c):
            hit = flat == src_local - x * (height * breadth)
            dp[level, x] = courant[x] * spatial(fp, level, x) + jnp.where(hit, amount, 0.0)
            return c

        lax.fori_loop(0, length, one, 0, unroll=2)

    def beyond(chain, level, side, i):
        total = None
        for k in range(i + 1, 5):
            at = 4 + i - k if side == 0 else k - i - 1
            term = STENCIL[k] * halo[chain, level, side, at]
            total = term if total is None else total + term
        return total

    def finish_q(level):
        for side in range(2):
            wait_halo(1, level, side)
            for i in range(4):
                x = i if side == 0 else length - 1 - i
                value = aq[x] + beyond(1, level, side, i)
                qs[level + 2][x] = value
                if level + 1 < steps:
                    fw[level + 1, x + 4] = courant[x] * value
            if level + 2 < steps:
                send_halo(1, level + 1, side)

    def finish_p(level):
        for side in range(2):
            wait_halo(0, level, side)
            for i in range(4):
                x = i if side == 0 else length - 1 - i
                change = dp[level, x] + courant[x] * beyond(0, level, side, i)
                if level + 1 < steps:
                    dp[level, x] = change
                    older = p0[x] if level == 0 else fp[level - 1, x + 4]
                    fp[level + 1, x + 4] = (2.0 * fp[level, x + 4] - older) + change
                else:
                    grad[x] = grad[x] + qs[1][x] * change
            if level + 1 < steps:
                send_halo(0, level + 1, side)

    def unpack(level, store):
        got = (in0, in1)[level]
        for off in range(1, n):
            a2a_copy(level, off).wait_recv()
        per_plane = height // 8

        def one(x, c):
            for r in range(per_plane):
                store(x, r, got[where[x * per_plane + r]])
            return c

        lax.fori_loop(0, length, one, 0)

    def store1(x, r, value):
        fp[0, x + 4, r * 8:(r + 1) * 8, :] = value

    def store0(x, r, value):
        p0[x, r * 8:(r + 1) * 8, :] = value

    prep_q(0)
    unpack(1, store1)
    for side in range(2):
        send_halo(0, 0, side)
    prep_p(0)
    finish_q(0)
    prep_q(1)
    unpack(0, store0)
    for level in range(steps - 1):
        finish_p(level)
        prep_p(level + 1)
        if level + 1 < steps - 1:
            finish_q(level + 1)
            prep_q(level + 2)

    def early(x, c):
        total = qs[steps][x] * dp[0, x]
        for m in range(1, steps - 1):
            total = total + qs[steps - m][x] * dp[m, x]
        grad[x] = total
        return c

    lax.fori_loop(0, length, early, 0)

    line = lax.broadcasted_iota(jnp.int32, (check_rows.shape[0], length * height), 1)
    chosen = check_rows[...]
    counts = jnp.zeros(line.shape, F32)
    for k in range(chosen.shape[1]):
        counts = counts + jnp.where(line == chosen[:, k:k + 1], 1.0, 0.0)
    counts = counts.astype(BF)

    finish_p(steps - 1)

    def rs_copy(off):
        peer = lax.rem(shot + off, shots)
        return pltpu.make_async_remote_copy(
            src_ref=grad.at[:, pl.ds(pl.multiple_of(peer * rows, rows), rows), :],
            dst_ref=rs.at[off],
            send_sem=rs_send.at[0, off],
            recv_sem=rs_recv.at[0, off],
            device_id={"shot": peer},
            device_id_type=MESH,
        )

    def rs_check_copy(off):
        peer = lax.rem(shot + off, shots)
        return pltpu.make_async_remote_copy(
            src_ref=check.at[pl.ds(pl.multiple_of(peer * check_each, check_each), check_each), :],
            dst_ref=rs_check.at[off],
            send_sem=rs_send.at[1, off],
            recv_sem=rs_recv.at[1, off],
            device_id={"shot": peer},
            device_id_type=MESH,
        )

    for off in range(1, shots):
        rs_copy(off).start()
    for side in range(2):
        send_halo(1, steps - 1, side)
    high, low = split(grad[...].reshape(length * height, breadth))
    both = dot(counts, jnp.concatenate([high, low], axis=1))
    check[...] = both[:, :breadth] + both[:, breadth:]
    for off in range(1, shots):
        rs_check_copy(off).start()

    finish_q(steps - 1)

    total = grad[:, pl.ds(pl.multiple_of(shot * rows, rows), rows), :]
    for off in range(1, shots):
        rs_copy(off).wait_recv()
        total = total + rs[off]
    grad_out[...] = total
    total = check[pl.ds(pl.multiple_of(shot * check_each, check_each), check_each), :]
    for off in range(1, shots):
        rs_check_copy(off).wait_recv()
        total = total + rs_check[off]
    check_out[...] = total

    for chain in range(2):
        for level in range(steps):
            for side in range(2):
                wait_sent(chain, level, side)
    for level in range(2):
        for off in range(1, n):
            a2a_copy(level, off).wait_send()
    for off in range(1, shots):
        rs_copy(off).wait_send()
        rs_check_copy(off).wait_send()


def tables(targets, n, cap, per_device, pos):
    grid = targets.reshape(n, per_device)
    peers = grid // per_device
    order = jnp.arange(per_device, dtype=jnp.int32)
    same = (peers[:, :, None] == peers[:, None, :]) & (order[None, None, :] < order[None, :, None])
    rank = jnp.sum(same.astype(jnp.int32), axis=2)
    sender = jnp.arange(n, dtype=jnp.int32)[:, None]
    slot = ((peers - sender + n) % n) * cap + rank
    own = lax.dynamic_index_in_dim(slot, pos, 0, keepdims=False)
    slots = jnp.arange(n * cap, dtype=jnp.int32)
    pack = jnp.sum(jnp.where(own[None, :] == slots[:, None], order[None, :], 0), axis=1)
    mine = pos * per_device + order
    where = jnp.sum(
        jnp.where(targets[None, :] == mine[:, None], slot.reshape(1, -1), 0), axis=1
    )
    return pack, where


def body(
    courant, checkpoint, block_target, adjoint_state, wavelet, source_cell,
    receiver_cell, residual, check_rows,
):
    n = lax.axis_size("space")
    shots = lax.axis_size("shot")
    length, height, breadth = courant.shape
    per_device = checkpoint.shape[2]
    cap = per_device // 4
    steps = wavelet.shape[1]
    chk = check_rows.shape[1]
    nrec = residual.shape[2]
    pack, where = tables(block_target[0], n, cap, per_device, lax.axis_index("space"))

    smem = pl.BlockSpec(memory_space=pltpu.SMEM)
    vmem = pl.BlockSpec(memory_space=pltpu.VMEM)
    slab = (length, height, breadth)
    buf = lambda *shape: pltpu.VMEM(shape, F32)
    blk = checkpoint.shape[3:]
    dma = pltpu.SemaphoreType.DMA
    grad, carry, check = pl.pallas_call(
        functools.partial(kernel, n, shots, cap),
        out_shape=(
            jax.ShapeDtypeStruct((length, height // shots, breadth), F32),
            jax.ShapeDtypeStruct((2,) + slab, F32),
            jax.ShapeDtypeStruct((chk // shots, breadth), F32),
        ),
        in_specs=[smem] * 4 + [vmem] * 6,
        out_specs=(vmem,) * 3,
        scratch_shapes=[
            buf(steps, length + 8, height, breadth),
            buf(steps, length + 8, height, breadth),
            buf(2, steps, 2, 4, height, breadth),
            buf(*slab), buf(*slab), buf(*slab), buf(*slab),
            buf(steps, *slab), buf(steps, *slab), buf(*slab),
            buf(chk, breadth),
            buf(shots, length, height // shots, breadth),
            buf(shots, chk // shots, breadth),
            buf(n * cap, *blk), buf(n * cap, *blk), buf(n * cap, *blk), buf(n * cap, *blk),
            pltpu.VMEM((2 * breadth, 2 * breadth), BF),
            pltpu.VMEM((2 * height, 2 * height), BF),
            pltpu.VMEM((steps * breadth, 2 * nrec), BF),
            dma((2, steps, 2)), dma((2, steps, 2)),
            dma((2, n)), dma((2, n)), dma((2, shots)), dma((2, shots)),
        ],
        compiler_params=pltpu.CompilerParams(
            collective_id=0, has_side_effects=True, vmem_limit_bytes=56 * 1024 * 1024
        ),
    )(
        pack, where, source_cell, wavelet[0],
        courant, checkpoint[0], adjoint_state[0], receiver_cell, residual[0], check_rows[0],
    )
    return grad, carry[None], check[None]


def solution(mesh):
    in_specs = (
        P("space", None, None),
        P("shot", None, "space", None, None),
        P("shot", None),
        P("shot", None, "space", None, None),
        P("shot", None),
        P("shot"),
        P("shot", None),
        P("shot", None, None),
        P("space", None, None),
    )
    out_specs = (
        P("space", "shot", None),
        P("shot", None, "space", None, None),
        P("space", "shot", None),
    )
    return jax.shard_map(body, mesh=mesh, in_specs=in_specs, out_specs=out_specs, check_vma=False)
```
